256 devices in a mesh: row: 32 (over z, x), col: 8 (over y, core).
Axes of the slice: x: 4, y: 4, z: 8, core: 2. Of those that a mesh axis runs over, the one named last changes fastest.
Arguments:
- x_dst: bfloat16 [32768, 256], P(('row', 'col')), may hold values from -96 to 96
- x_src: bfloat16 [8, 8192, 256], P('col', 'row'), may hold values from -96 to 96
- w_query: bfloat16 [256, 256], replicated, may hold values from -0.375 to 0.375
- w_key: bfloat16 [256, 256], replicated, may hold values from -0.375 to 0.375
- w_value: bfloat16 [256, 256], replicated, may hold values from -0.375 to 0.375
- w_out: bfloat16 [256, 256], replicated, may hold values from -1.5 to 1.5
- sink: float32 [8], replicated, may hold values from 2 to 8
- node_order: int32 [8, 8192], P('col'), may hold values from 0 to 8191, each once within a row
- tile_coords: int32 [32, 8, 2, 128], P('row', 'col'), may hold values from 0 to 63, as said below
- tile_count: int32 [32, 8], P('row', 'col'), may hold values from 32 to 128, as said below
- edge_mask: int32 [32, 8, 128, 128, 128], P('row', 'col'), may hold values 0 or 1
Outputs:
- attended: bfloat16 [32768, 256], P(('row', 'col'))
The draws below stay inside these ranges and needn't reach their ends.
Inputs may be any that keep to these rules, and one draw needn't show every extreme that they name: tile_coords[r, c, 0, t] is a destination block below 8, tile_coords[r, c, 1, t] a source block below 64; the 128 pairs of one device are distinct. `tile_count`: some device uses all 128 slots in every draw. `node_order`: each row is a permutation.
All inputs are finite; a program needn't handle non-finite values. No bound on the sum of `edge_mask` on one device may be relied on, other than what follows from the above.
Results may differ from the reference program's by a relative error of at most 0.02195.
The reference program's roundings to bfloat16 on the way count: a program that leaves them out, or rounds other values in their place, can miss the bound.
Values may be sent and summed in bfloat16 or wider, within the bound.
A program may use at most 128 MiB of HBM per device.

```python
import math
import jax
import jax.numpy as jnp
from jax import lax

D = 256
HEADS = 8
HD = 32
TILE = 128
DB_GRP = 8
SB_GRP = 64
CSRC = 8192
NDST = 32768
NT = 128
N_ROW = 32
N_COL = 8


def scaled_rows(key, shape):
    base = jnp.clip(jax.random.normal(key, shape, jnp.float32), -6.0, 6.0)
    return base.astype(jnp.bfloat16)


def draw_x_dst(key, part):
    key = jax.random.fold_in(key, 1)
    return scaled_rows(key, (NDST, D))


def draw_x_src(key, part):
    key = jax.random.fold_in(key, 2)
    return scaled_rows(key, (N_COL, CSRC, D))


def draw_tile_coords(key, part):
    key = jax.random.fold_in(key, 3)
    keys = jax.random.split(key, N_ROW * N_COL)
    picks = jax.vmap(lambda one: jax.random.permutation(one, DB_GRP * SB_GRP)[:NT])(keys)
    stacked = jnp.stack([picks // SB_GRP, picks % SB_GRP], axis=1)
    return stacked.reshape(N_ROW, N_COL, 2, NT).astype(jnp.int32)


def draw_tile_count(key, part):
    key = jax.random.fold_in(key, 4)
    divisor = jax.random.randint(key, (N_ROW * N_COL,), 1, 5)
    counts = NT // divisor
    busiest = jax.random.randint(jax.random.fold_in(key, 9), (), 0, N_ROW * N_COL)
    counts = jnp.where(jnp.arange(N_ROW * N_COL) == busiest, NT, counts)
    return counts.reshape(N_ROW, N_COL).astype(jnp.int32)


def with_ends(drawn, rng, smallest, largest):
    dims = drawn.shape
    place = [jax.random.randint(jax.random.fold_in(rng, axis), (), 0, dims[axis]) for axis in range(len(dims))]
    drawn = drawn.at[tuple(place)].set(smallest)
    longest = dims.index(max(dims))
    place[longest] = (place[longest] + 1) % dims[longest]
    return drawn.at[tuple(place)].set(largest)


def normal_values(stream_key, extent, deviation, bound, kind=jnp.bfloat16):
    values = jax.random.normal(stream_key, extent, jnp.float32) * deviation
    return jnp.minimum(jnp.maximum(values, -bound), bound).astype(kind)


def setup_inputs(seed: int = 0) -> dict:
    key_list = jax.random.split(jax.random.key(seed), 12)
    return {
        "x_dst": draw_x_dst(jax.random.fold_in(key_list[11], 71), 0),
        "x_src": draw_x_src(jax.random.fold_in(key_list[11], 71), 0),
        "w_query": normal_values(key_list[2], (D, D), D ** -0.5, 0.375),
        "w_key": normal_values(key_list[3], (D, D), D ** -0.5, 0.375),
        "w_value": normal_values(key_list[4], (D, D), D ** -0.5, 0.375),
        "w_out": normal_values(key_list[5], (D, D), (D // 16) ** -0.5, 1.5),
        "sink": jnp.clip(jax.random.uniform(key_list[6], (HEADS,), jnp.float32, 2.0, 8.0), 2.0, 8.0),
        "node_order": jax.vmap(lambda own: jax.random.permutation(own, CSRC))(jax.random.split(key_list[7], N_COL)).reshape((N_COL, CSRC)).astype(jnp.int32),
        "tile_coords": draw_tile_coords(jax.random.fold_in(key_list[11], 71), 0),
        "tile_count": draw_tile_count(jax.random.fold_in(key_list[11], 71), 0),
        "edge_mask": with_ends((jax.random.randint(key_list[10], (N_ROW, N_COL, NT, TILE, TILE), 0, 16) < 1).astype(jnp.int32), jax.random.fold_in(key_list[10], 1), 0, 1),
    }


def reference(x_dst, x_src, w_query, w_key, w_value, w_out, sink, node_order, tile_coords, tile_count, edge_mask):
    scale = 1.0 / math.sqrt(HD)
    query = jnp.dot(x_dst, w_query, preferred_element_type=jnp.float32).astype(jnp.bfloat16)
    flat_src = x_src.reshape(N_COL * CSRC, D)
    keys = jnp.dot(flat_src, w_key, preferred_element_type=jnp.float32).astype(jnp.bfloat16).reshape(N_COL, CSRC, D)
    values = jnp.dot(flat_src, w_value, preferred_element_type=jnp.float32).astype(jnp.bfloat16).reshape(N_COL, CSRC, D)
    keys = jnp.take_along_axis(keys, node_order[:, :, None], axis=1)
    values = jnp.take_along_axis(values, node_order[:, :, None], axis=1)
    query_blocks = query.reshape(N_ROW, DB_GRP, TILE, HEADS, HD)
    key_blocks = keys.reshape(N_COL, SB_GRP, TILE, HEADS, HD)
    value_blocks = values.reshape(N_COL, SB_GRP, TILE, HEADS, HD)

    def device_scores(index):
        row_idx = index // N_COL
        col_idx = index % N_COL
        coords = tile_coords[row_idx, col_idx]
        live = jnp.arange(NT, dtype=jnp.int32) < tile_count[row_idx, col_idx]
        edges = (edge_mask[row_idx, col_idx] == 1) & live[:, None, None]
        q_tiles = query_blocks[row_idx][coords[0]].astype(jnp.float32)
        k_tiles = key_blocks[col_idx][coords[1]].astype(jnp.float32)
        scores = jnp.einsum('tihd,tjhd->thij', q_tiles, k_tiles) * scale
        return (row_idx, col_idx, coords, edges[:, None], scores)

    def pass_max(maxima, index):
        row_idx, col_idx, coords, edges, scores = device_scores(index)
        rowmax = lax.optimization_barrier(jnp.max(jnp.where(edges, scores, -1e+30), axis=3))
        return (maxima.at[row_idx, coords[0]].max(rowmax), None)
    devices = jnp.arange(N_ROW * N_COL, dtype=jnp.int32)
    start = jnp.full((N_ROW, DB_GRP, HEADS, TILE), -1e+30, jnp.float32)
    maxima, unused = lax.scan(pass_max, start, devices)
    top = jnp.maximum(maxima, sink[None, None, :, None])

    def pass_sum(carry, index):
        acc, total = carry
        row_idx, col_idx, coords, edges, scores = device_scores(index)
        shift = top[row_idx][coords[0]][..., None]
        weights = jnp.exp(jnp.where(edges, scores - shift, -1e+30))
        total = total.at[row_idx, coords[0]].add(lax.optimization_barrier(jnp.sum(weights, axis=3)))
        rounded = lax.optimization_barrier(weights.astype(jnp.bfloat16)).astype(jnp.float32)
        v_tiles = value_blocks[col_idx][coords[1]].astype(jnp.float32)
        mixed = jnp.einsum('thij,tjhd->tihd', rounded, v_tiles).reshape(NT, TILE, D)
        acc = acc.at[row_idx, coords[0]].add(mixed)
        return ((acc, total), None)
    init = (jnp.zeros((N_ROW, DB_GRP, TILE, D), jnp.float32), jnp.zeros((N_ROW, DB_GRP, HEADS, TILE), jnp.float32))
    (acc, total), unused = lax.scan(pass_sum, init, devices)
    denom = total + jnp.exp(sink[None, None, :, None] - top)
    mixed = acc.reshape(N_ROW, DB_GRP, TILE, HEADS, HD) / jnp.transpose(denom, (0, 1, 3, 2))[..., None]
    mixed = mixed.reshape(NDST, D).astype(jnp.bfloat16)
    return jnp.dot(mixed, w_out, preferred_element_type=jnp.float32).astype(jnp.bfloat16)
```

```python
import functools
import math

import jax
import jax.numpy as jnp
from jax import lax
from jax.experimental import pallas as pl
from jax.experimental.pallas import tpu as pltpu
from jax.sharding import PartitionSpec as P

MASKED = -1e30
UNROLL = 8
TILE = 128


def dot_nt(a, b):
    return lax.dot_general(a, b, (((1,), (1,)), ((), ())), preferred_element_type=jnp.float32)


def attend_kernel(
    order_ref, coords_ref, count_ref, sink_ref, x_ref, q_ref, wk_ref, wvt_ref, bias_hbm,
    acc_out, stat_out,
    rows, lo, hi, keys, values, qz, acc, top, total, bias, sbuf, peak, sem,
):
    heads = sink_ref.shape[0]
    n_dblk, width, tile = q_ref.shape
    hd = width // heads
    half = width // 2
    per_half = heads // 2
    c = math.log2(math.e) / math.sqrt(hd)
    nsrc = x_ref.shape[0]
    nblk = nsrc // tile
    slots = bias_hbm.shape[0]
    count = count_ref[0]
    load = pltpu.make_async_copy(bias_hbm, bias.at[pl.ds(0, slots)], sem.at[0])
    load.start()

    @pl.loop(0, nsrc // 256)
    def _(i):
        r = pl.ds(pl.multiple_of(i * 256, 256), 256)
        v = x_ref[r, :].astype(jnp.float32)
        rows[0, r, :] = v[:, :half]
        rows[1, r, :] = v[:, half:]

    qz[...] = jnp.zeros_like(qz)
    for d in range(n_dblk):
        for h in range(heads):
            hh = h % per_half
            qz[d, hh * hd:(hh + 1) * hd, h * tile:(h + 1) * tile] = q_ref[d, h * hd:(h + 1) * hd, :]

    bias[slots] = jnp.full(bias.shape[1:], MASKED, jnp.bfloat16)
    acc[...] = jnp.zeros_like(acc)
    total[...] = jnp.zeros_like(total)
    for d in range(n_dblk):
        for h in range(heads):
            top[d, h:h + 1, :] = jnp.full((1, tile), sink_ref[h] * math.sqrt(hd), jnp.float32)

    wk = wk_ref[...]
    wvt = wvt_ref[...]

    def gather(b, e):
        base = b * tile
        for r in range(tile):
            idx = order_ref[base + r]
            lo[e, r:r + 1, :] = rows[0, pl.ds(idx, 1), :]
            hi[e, r:r + 1, :] = rows[1, pl.ds(idx, 1), :]

    def project(b, e):
        x = jnp.concatenate([lo[e].astype(jnp.bfloat16), hi[e].astype(jnp.bfloat16)], axis=1)
        keys[b] = jnp.dot(x, wk, preferred_element_type=jnp.float32).astype(jnp.bfloat16)
        values[b] = dot_nt(wvt, x).astype(jnp.bfloat16)

    gather(0, 0)

    @pl.loop(0, nblk // 2)
    def _(i):
        gather(2 * i + 1, 1)
        project(2 * i, 0)
        gather(jnp.minimum(2 * i + 2, nblk - 1), 0)
        project(2 * i + 1, 1)

    load.wait()
    ones = jnp.ones((16, tile), jnp.bfloat16)

    def place(t):
        u = jnp.minimum(t, slots - 1)
        return coords_ref[0, u], coords_ref[1, u]

    def scores(t, e):
        d, b = place(t)
        bt = bias[jnp.where(t < count, t, slots)].astype(jnp.float32)
        for hp in range(heads // 2):
            g = 2 * hp // per_half
            pair = jnp.dot(
                keys[b, :, g * half:(g + 1) * half],
                qz[d, :, 2 * hp * tile:2 * (hp + 1) * tile],
                preferred_element_type=jnp.float32,
            )
            for i in range(2):
                s = pair[:, i * tile:(i + 1) * tile] + bt
                sbuf[e, 2 * hp + i] = s
                peak[e, 2 * hp + i:2 * hp + i + 1, :] = jnp.max(s, axis=0, keepdims=True)

    def weigh(t, e):
        d, b = place(t)
        before = top[d]
        now = jnp.maximum(before, peak[e])
        fade = jnp.exp2((before - now) * c)
        top[d] = now
        sums = []
        for h in range(heads):
            f = slice(h * hd, (h + 1) * hd)
            p = jnp.exp2((sbuf[e, h] - now[h:h + 1]) * c).astype(jnp.bfloat16)
            v = jnp.concatenate([values[b, f, :], ones], axis=0)
            o = jnp.dot(v, p, preferred_element_type=jnp.float32)
            acc[d, f, :] = acc[d, f, :] * fade[h:h + 1] + o[:hd]
            sums.append(o[hd:hd + 1])
        total[d] = total[d] * fade + jnp.concatenate(sums, axis=0)

    scores(0, 0)

    @pl.loop(0, (count + UNROLL - 1) // UNROLL)
    def _(i):
        for u in range(UNROLL):
            t = i * UNROLL + u
            scores(t + 1, (u + 1) % 2)
            weigh(t, u % 2)

    acc_out[...] = acc[...].astype(jnp.bfloat16)
    for d in range(n_dblk):
        stat_out[d, :heads, :] = top[d] * c
        stat_out[d, heads:, :] = total[d]


def attend(order, coords, count, sink, x, q, wk, wvt, bias):
    nsrc, width = x.shape
    n_dblk, _, tile = q.shape
    heads = sink.shape[0]
    slots = bias.shape[0]
    nblk = nsrc // tile
    smem = pl.BlockSpec(memory_space=pltpu.SMEM)
    vmem = pl.BlockSpec(memory_space=pltpu.VMEM)
    return pl.pallas_call(
        attend_kernel,
        out_shape=(
            jax.ShapeDtypeStruct((n_dblk, width, tile), jnp.bfloat16),
            jax.ShapeDtypeStruct((n_dblk, 2 * heads, tile), jnp.float32),
        ),
        in_specs=[smem] * 4 + [vmem] * 4 + [pl.BlockSpec(memory_space=pl.ANY)],
        out_specs=(vmem, vmem),
        scratch_shapes=[
            pltpu.VMEM((2, nsrc, width // 2), jnp.float32),
            pltpu.VMEM((2, tile, width // 2), jnp.float32),
            pltpu.VMEM((2, tile, width // 2), jnp.float32),
            pltpu.VMEM((nblk, tile, width), jnp.bfloat16),
            pltpu.VMEM((nblk, width, tile), jnp.bfloat16),
            pltpu.VMEM((n_dblk, width // 2, heads * tile), jnp.bfloat16),
            pltpu.VMEM((n_dblk, width, tile), jnp.float32),
            pltpu.VMEM((n_dblk, heads, tile), jnp.float32),
            pltpu.VMEM((n_dblk, heads, tile), jnp.float32),
            pltpu.VMEM((slots + 1, tile, tile), jnp.bfloat16),
            pltpu.VMEM((2, heads, tile, tile), jnp.float32),
            pltpu.VMEM((2, heads, tile), jnp.float32),
            pltpu.SemaphoreType.DMA((1,)),
        ],
        compiler_params=pltpu.CompilerParams(vmem_limit_bytes=56 * 2**20),
        name="attend",
    )(order, coords, count, sink, x, q, wk, wvt, bias)


def body(
    x_dst, x_src, w_query, w_key, w_value, w_out, sink, node_order, tile_coords, tile_count, edge_mask
):
    heads = sink.shape[0]
    width = x_dst.shape[1]
    hd = width // heads
    tile = edge_mask.shape[-1]
    x = lax.all_gather(x_src[0], "row", axis=0, tiled=True)
    q_own = dot_nt(w_query.T, x_dst).astype(jnp.bfloat16)
    q = lax.all_gather(q_own, "col", axis=0)
    bias = jnp.where(edge_mask[0, 0] == 1, 0.0, MASKED).astype(jnp.bfloat16).swapaxes(1, 2)
    acc, stat = attend(
        node_order[0], tile_coords[0, 0], tile_count[0], sink, x, q, w_key, w_value.T, bias
    )
    acc = lax.all_to_all(acc, "col", 0, 0).astype(jnp.float32)
    stat = lax.all_to_all(stat, "col", 0, 0)
    tops, totals = stat[:, :heads], stat[:, heads:]
    top = jnp.max(tops, axis=0)
    fade = jnp.exp2(tops - top)
    denom = jnp.sum(totals * fade, axis=0) + jnp.exp2(sink[:, None] * math.log2(math.e) - top)
    acc = jnp.sum(acc.reshape(-1, heads, hd, tile) * fade[:, :, None, :], axis=0)
    mixed = (acc / denom[:, None, :]).reshape(width, tile).T.astype(jnp.bfloat16)
    return jnp.dot(mixed, w_out, preferred_element_type=jnp.float32).astype(jnp.bfloat16)


def solution(mesh):
    in_specs = (
        P(("row", "col"), None),
        P("col", "row", None),
        P(),
        P(),
        P(),
        P(),
        P(),
        P("col", None),
        P("row", "col", None, None),
        P("row", "col"),
        P("row", "col", None, None, None),
    )
    out_specs = P(("row", "col"), None)
    return jax.shard_map(body, mesh=mesh, in_specs=in_specs, out_specs=out_specs, check_vma=False)
```

```python
import functools
import math

import jax
import jax.numpy as jnp
from jax import lax
from jax.experimental import pallas as pl
from jax.experimental.pallas import tpu as pltpu
from jax.sharding import PartitionSpec as P

MASKED = -1e30
UNROLL = 8
TILE = 128


def dot_nt(a, b):
    return lax.dot_general(a, b, (((1,), (1,)), ((), ())), preferred_element_type=jnp.float32)


MESH = pl.DeviceIdType.MESH
LINKS = ("x+", "x-", "z+", "z-")
STEP = {"x+": (1, 0), "x-": (-1, 0), "z+": (0, 1), "z-": (0, -1)}
SPLIT = 96


def spread_plan(nx, nz, rows):
    cut = {"A": (0, SPLIT // 2, SPLIT), "B": (SPLIT, (SPLIT + rows) // 2, rows)}
    sends, events, free, pending = [], [], {link: 0.0 for link in LINKS}, []

    def issue(now, kind, link, ox, oz, lo, hi):
        if hi <= lo:
            return
        start = max(free[link], now)
        free[link] = start + (hi - lo)
        pending.append((free[link] + 60.0, len(sends), kind))
        sends.append((link, ox, oz, lo, hi - lo))
        events.append(("send", len(sends) - 1))

    def clip(kind, link, k, half, lo, hi):
        if k + 1 < half:
            return lo, hi
        if k + 1 > half:
            return lo, lo
        a, m, b = cut[kind]
        return (max(lo, a), min(hi, m)) if link[1] == "+" else (max(lo, m), min(hi, b))

    for kind, order in (("B", ("z+", "z-")), ("A", ("x+", "x-")), ("A", ("z+", "z-")), ("B", ("x+", "x-"))):
        for link in order:
            issue(0.0, kind, link, 0, 0, cut[kind][0], cut[kind][2])
    while pending:
        pending.sort()
        now, k, kind = pending.pop(0)
        link, ox, oz, lo, n = sends[k]
        hi = lo + n
        events.append(("recv", k))
        ox, oz = ox - STEP[link][0], oz - STEP[link][1]
        on_x = link[0] == "x"
        first = on_x == (kind == "A")
        far, half = (abs(ox), nx // 2) if on_x else (abs(oz), nz // 2)
        a, b = clip(kind, link, far, half, lo, hi)
        issue(now, kind, link, ox, oz, a, b)
        if first:
            for other in ("z+", "z-") if on_x else ("x+", "x-"):
                a, b = clip(kind, other, 0, nz // 2 if on_x else nx // 2, lo, hi)
                issue(now, kind, other, ox, oz, a, b)
    return sends, events


def gather_kernel(
    nx, nz, ncol, sends, events,
    x_dst, w_query, x_src, mask_hbm,
    x_all, q_all, bias_hbm,
    q_own, masks, bias, send_sem, recv_sem, q_send, q_recv, in_sem, out_sem, own_sem,
):
    row, col = lax.axis_index("row"), lax.axis_index("col")
    z, x = row // nx, lax.rem(row, nx)
    slots = masks.shape[0]
    chunks = in_sem.shape[0]
    per = slots // chunks

    def loaded(i):
        part = pl.ds(i * per, per)
        return pltpu.make_async_copy(mask_hbm.at[part], masks.at[part], in_sem.at[i])

    def stored(i):
        part = pl.ds(i * per, per)
        return pltpu.make_async_copy(bias.at[part], bias_hbm.at[part], out_sem.at[i])

    def at(ox, oz):
        return lax.rem(z + oz + nz, nz) * nx + lax.rem(x + ox + nx, nx)

    def peer(o):
        return lax.rem(col + o, ncol)

    barrier = pltpu.get_barrier_semaphore()
    for link in LINKS:
        pl.semaphore_signal(barrier, inc=1, device_id={"row": at(*STEP[link])}, device_id_type=MESH)
    for o in range(1, ncol):
        pl.semaphore_signal(barrier, inc=1, device_id={"col": peer(o)}, device_id_type=MESH)
    for i in range(chunks):
        loaded(i).start()
    own_x = pltpu.make_async_copy(x_src, x_all.at[row], own_sem.at[0])
    own_x.start()
    pl.semaphore_wait(barrier, len(LINKS) + ncol - 1)

    def piece(k, arriving):
        link, ox, oz, lo, n = sends[k]
        dx, dz = STEP[link]
        origin = at(ox - dx, oz - dz) if arriving else at(ox, oz)
        part = pl.ds(lo, n)
        own = ox == 0 and oz == 0 and not arriving
        return pltpu.make_async_remote_copy(
            src_ref=x_src.at[part] if own else x_all.at[origin, part],
            dst_ref=x_all.at[origin, part],
            send_sem=send_sem.at[k],
            recv_sem=recv_sem.at[k],
            device_id={"row": at(dx, dz)},
            device_id_type=MESH,
        )

    def query(o, slot):
        return pltpu.make_async_remote_copy(
            src_ref=q_own,
            dst_ref=q_all.at[slot],
            send_sem=q_send.at[o - 1],
            recv_sem=q_recv.at[o - 1],
            device_id={"col": peer(o)},
            device_id_type=MESH,
        )

    share = -(-slots // (len(sends) - 8))

    def turn(first, last):
        @pl.loop(first, last)
        def _(t):
            bias[t] = jnp.where(masks[t] == 1, 0.0, MASKED).T.astype(jnp.bfloat16)

    def work(first, last):
        for i in range(chunks):
            if first <= i * per < last:
                loaded(i).wait()
        turn(first, last)
        for i in range(chunks):
            if first < (i + 1) * per <= last:
                stored(i).start()

    own_q = None
    done = 0
    for n, (what, k) in enumerate(events):
        if what == "send":
            piece(k, False).start()
        else:
            if own_q is None:
                q = jnp.dot(x_dst[...], w_query[...], preferred_element_type=jnp.float32)
                q_own[...] = q.T.astype(jnp.bfloat16)
                for o in range(1, ncol):
                    query(o, col).start()
                own_q = pltpu.make_async_copy(q_own, q_all.at[col], own_sem.at[1])
                own_q.start()
            piece(k, True).wait_recv()
        if own_q is not None and done < slots and events[n + 1][0] == "recv":
            end = min(slots, done + share)
            work(done, end)
            done = end
    for o in range(1, ncol):
        query(o, lax.rem(col - o + ncol, ncol)).wait_recv()
    for k in range(len(sends)):
        piece(k, False).wait_send()
    for o in range(1, ncol):
        query(o, col).wait_send()
    for i in range(chunks):
        stored(i).wait()
    own_x.wait()
    own_q.wait()


def gather_all(nx, nz, ncol, x_dst, w_query, x_src, mask):
    rows, width = x_src.shape
    slots, tile, _ = mask.shape
    sends, events = spread_plan(nx, nz, rows)
    vmem = pl.BlockSpec(memory_space=pltpu.VMEM)
    hbm = pl.BlockSpec(memory_space=pl.ANY)
    dma = pltpu.SemaphoreType.DMA
    return pl.pallas_call(
        functools.partial(gather_kernel, nx, nz, ncol, sends, events),
        out_shape=(
            jax.ShapeDtypeStruct((nx * nz, rows, width), jnp.bfloat16),
            jax.ShapeDtypeStruct((ncol, width, x_dst.shape[0]), jnp.bfloat16),
            jax.ShapeDtypeStruct(mask.shape, jnp.bfloat16),
        ),
        in_specs=[vmem, vmem, hbm, hbm],
        out_specs=(hbm, hbm, hbm),
        scratch_shapes=[
            pltpu.VMEM((width, x_dst.shape[0]), jnp.bfloat16),
            pltpu.VMEM(mask.shape, jnp.int32),
            pltpu.VMEM(mask.shape, jnp.bfloat16),
            dma((len(sends),)),
            dma((len(sends),)),
            dma((ncol - 1,)),
            dma((ncol - 1,)),
            dma((16,)),
            dma((16,)),
            dma((2,)),
        ],
        compiler_params=pltpu.CompilerParams(
            collective_id=0, has_side_effects=True, vmem_limit_bytes=32 * 2**20
        ),
        name="gather_all",
    )(x_dst, w_query, x_src, mask)


def attend_kernel(
    order_ref, coords_ref, count_ref, sink_ref, x_ref, q_ref, wk_ref, wv_ref, bias_hbm,
    acc_out, stat_out,
    rows, lo, hi, keys, values, qz, acc, top, total, bias, sbuf, peak, sem,
):
    heads = sink_ref.shape[0]
    n_dblk, width, tile = q_ref.shape
    hd = width // heads
    half = width // 2
    per_half = heads // 2
    c = math.log2(math.e) / math.sqrt(hd)
    nsrc = x_ref.shape[0]
    nblk = nsrc // tile
    slots = bias_hbm.shape[0]
    count = count_ref[0]
    load = pltpu.make_async_copy(bias_hbm, bias.at[pl.ds(0, slots)], sem.at[0])
    load.start()

    @pl.loop(0, nsrc // 256)
    def _(i):
        r = pl.ds(pl.multiple_of(i * 256, 256), 256)
        v = x_ref[r, :].astype(jnp.float32)
        rows[0, r, :] = v[:, :half]
        rows[1, r, :] = v[:, half:]

    qz[...] = jnp.zeros_like(qz)
    for d in range(n_dblk):
        for h in range(heads):
            hh = h % per_half
            qz[d, hh * hd:(hh + 1) * hd, h * tile:(h + 1) * tile] = q_ref[d, h * hd:(h + 1) * hd, :]

    bias[slots] = jnp.full(bias.shape[1:], MASKED, jnp.bfloat16)
    acc[...] = jnp.zeros_like(acc)
    total[...] = jnp.zeros_like(total)
    for d in range(n_dblk):
        for h in range(heads):
            top[d, h:h + 1, :] = jnp.full((1, tile), sink_ref[h] * math.sqrt(hd), jnp.float32)

    wk = wk_ref[...]
    wvt = wv_ref[...].astype(jnp.float32).T.astype(jnp.bfloat16)

    def gather(b, e):
        base = b * tile
        for r in range(tile):
            idx = order_ref[base + r]
            lo[e, r:r + 1, :] = rows[0, pl.ds(idx, 1), :]
            hi[e, r:r + 1, :] = rows[1, pl.ds(idx, 1), :]

    def project(b, e):
        x = jnp.concatenate([lo[e].astype(jnp.bfloat16), hi[e].astype(jnp.bfloat16)], axis=1)
        keys[b] = jnp.dot(x, wk, preferred_element_type=jnp.float32).astype(jnp.bfloat16)
        values[b] = dot_nt(wvt, x).astype(jnp.bfloat16)

    gather(0, 0)

    @pl.loop(0, nblk // 2)
    def _(i):
        gather(2 * i + 1, 1)
        project(2 * i, 0)
        gather(jnp.minimum(2 * i + 2, nblk - 1), 0)
        project(2 * i + 1, 1)

    load.wait()
    ones = jnp.ones((16, tile), jnp.bfloat16)

    def place(t):
        u = jnp.minimum(t, slots - 1)
        return coords_ref[0, u], coords_ref[1, u]

    def scores(t, e):
        d, b = place(t)
        bt = bias[jnp.where(t < count, t, slots)].astype(jnp.float32)
        for hp in range(heads // 2):
            g = 2 * hp // per_half
            pair = jnp.dot(
                keys[b, :, g * half:(g + 1) * half],
                qz[d, :, 2 * hp * tile:2 * (hp + 1) * tile],
                preferred_element_type=jnp.float32,
            )
            for i in range(2):
                s = pair[:, i * tile:(i + 1) * tile] + bt
                sbuf[e, 2 * hp + i] = s
                peak[e, 2 * hp + i:2 * hp + i + 1, :] = jnp.max(s, axis=0, keepdims=True)

    def weigh(t, e):
        d, b = place(t)
        before = top[d]
        now = jnp.maximum(before, peak[e])
        fade = jnp.exp2((before - now) * c)
        top[d] = now
        sums = []
        for h in range(heads):
            f = slice(h * hd, (h + 1) * hd)
            p = jnp.exp2((sbuf[e, h] - now[h:h + 1]) * c).astype(jnp.bfloat16)
            v = jnp.concatenate([values[b, f, :], ones], axis=0)
            o = jnp.dot(v, p, preferred_element_type=jnp.float32)
            acc[d, f, :] = acc[d, f, :] * fade[h:h + 1] + o[:hd]
            sums.append(o[hd:hd + 1])
        total[d] = total[d] * fade + jnp.concatenate(sums, axis=0)

    scores(0, 0)

    @pl.loop(0, (count + UNROLL - 1) // UNROLL)
    def _(i):
        for u in range(UNROLL):
            t = i * UNROLL + u
            scores(t + 1, (u + 1) % 2)
            weigh(t, u % 2)

    acc_out[...] = acc[...].astype(jnp.bfloat16)
    for d in range(n_dblk):
        stat_out[d, :heads, :] = top[d] * c
        stat_out[d, heads:, :] = total[d]


def attend(order, coords, count, sink, x, q, wk, wv, bias):
    nsrc, width = x.shape
    n_dblk, _, tile = q.shape
    heads = sink.shape[0]
    slots = bias.shape[0]
    nblk = nsrc // tile
    smem = pl.BlockSpec(memory_space=pltpu.SMEM)
    vmem = pl.BlockSpec(memory_space=pltpu.VMEM)
    return pl.pallas_call(
        attend_kernel,
        out_shape=(
            jax.ShapeDtypeStruct((n_dblk, width, tile), jnp.bfloat16),
            jax.ShapeDtypeStruct((n_dblk, 2 * heads, tile), jnp.float32),
        ),
        in_specs=[smem] * 4 + [vmem] * 4 + [pl.BlockSpec(memory_space=pl.ANY)],
        out_specs=(vmem, vmem),
        scratch_shapes=[
            pltpu.VMEM((2, nsrc, width // 2), jnp.float32),
            pltpu.VMEM((2, tile, width // 2), jnp.float32),
            pltpu.VMEM((2, tile, width // 2), jnp.float32),
            pltpu.VMEM((nblk, tile, width), jnp.bfloat16),
            pltpu.VMEM((nblk, width, tile), jnp.bfloat16),
            pltpu.VMEM((n_dblk, width // 2, heads * tile), jnp.bfloat16),
            pltpu.VMEM((n_dblk, width, tile), jnp.float32),
            pltpu.VMEM((n_dblk, heads, tile), jnp.float32),
            pltpu.VMEM((n_dblk, heads, tile), jnp.float32),
            pltpu.VMEM((slots + 1, tile, tile), jnp.bfloat16),
            pltpu.VMEM((2, heads, tile, tile), jnp.float32),
            pltpu.VMEM((2, heads, tile), jnp.float32),
            pltpu.SemaphoreType.DMA((1,)),
        ],
        compiler_params=pltpu.CompilerParams(vmem_limit_bytes=56 * 2**20),
        name="attend",
    )(order, coords, count, sink, x, q, wk, wv, bias)


def finish_kernel(ncol, sink_ref, acc_ref, stat_ref, w_out, out_ref, accs, stats, a_send, a_recv, s_send, s_recv):
    col = lax.axis_index("col")
    heads = sink_ref.shape[0]
    _, width, tile = acc_ref.shape
    hd = width // heads

    def peer(o):
        return lax.rem(col + o, ncol)

    barrier = pltpu.get_barrier_semaphore()
    for o in range(1, ncol):
        pl.semaphore_signal(barrier, inc=1, device_id={"col": peer(o)}, device_id_type=MESH)
    pl.semaphore_wait(barrier, ncol - 1)

    moves = ((stat_ref, stats, s_send, s_recv), (acc_ref, accs, a_send, a_recv))

    def copy(o, which):
        src, dst, send, recv = moves[which]
        return pltpu.make_async_remote_copy(
            src_ref=src.at[peer(o)],
            dst_ref=dst.at[o - 1],
            send_sem=send.at[o - 1],
            recv_sem=recv.at[o - 1],
            device_id={"col": peer(o)},
            device_id_type=MESH,
        )

    order = sorted(range(1, ncol), key=lambda o: -min(o, ncol - o))
    for o in order:
        copy(o, 0).start()
        copy(o, 1).start()
    stat = [stat_ref[col]]
    for o in range(1, ncol):
        copy(o, 0).wait_recv()
        stat.append(stats[o - 1])
    top = functools.reduce(jnp.maximum, [s[:heads] for s in stat])
    fades = [jnp.exp2(s[:heads] - top) for s in stat]
    sinks = jnp.concatenate([jnp.full((1, tile), sink_ref[h] * math.log2(math.e), jnp.float32) for h in range(heads)], axis=0)
    total = jnp.exp2(sinks - top)
    for s, fade in zip(stat, fades):
        total = total + s[heads:] * fade

    def spread(per_head):
        return jnp.concatenate([jnp.broadcast_to(per_head[h:h + 1], (hd, tile)) for h in range(heads)], axis=0)

    mixed = acc_ref[col].astype(jnp.float32) * spread(fades[0])
    for o in range(1, ncol):
        copy(o, 1).wait_recv()
        mixed = mixed + accs[o - 1].astype(jnp.float32) * spread(fades[o])
    mixed = (mixed / spread(total)).T.astype(jnp.bfloat16)
    out_ref[...] = jnp.dot(mixed, w_out[...], preferred_element_type=jnp.float32).astype(jnp.bfloat16)
    for o in range(1, ncol):
        copy(o, 0).wait_send()
        copy(o, 1).wait_send()


def finish(sink, acc, stat, w_out):
    ncol, width, tile = acc.shape
    vmem = pl.BlockSpec(memory_space=pltpu.VMEM)
    dma = pltpu.SemaphoreType.DMA
    return pl.pallas_call(
        functools.partial(finish_kernel, ncol),
        out_shape=jax.ShapeDtypeStruct((tile, width), jnp.bfloat16),
        in_specs=[pl.BlockSpec(memory_space=pltpu.SMEM), vmem, vmem, vmem],
        out_specs=vmem,
        scratch_shapes=[
            pltpu.VMEM((ncol - 1, width, tile), jnp.bfloat16),
            pltpu.VMEM((ncol - 1,) + stat.shape[1:], jnp.float32),
        ]
        + [dma((ncol - 1,))] * 4,
        compiler_params=pltpu.CompilerParams(
            collective_id=1, has_side_effects=True, vmem_limit_bytes=16 * 2**20
        ),
        name="finish",
    )(sink, acc, stat, w_out)


def body(
    nx, nz, ncol,
    x_dst, x_src, w_query, w_key, w_value, w_out, sink, node_order, tile_coords, tile_count, edge_mask,
):
    x, q, bias = gather_all(nx, nz, ncol, x_dst, w_query, x_src[0], edge_mask[0, 0])
    acc, stat = attend(
        node_order[0], tile_coords[0, 0], tile_count[0], sink, x.reshape(-1, x.shape[-1]), q, w_key, w_value, bias
    )
    return finish(sink, acc, stat, w_out)


NX = 4


def solution(mesh):
    in_specs = (
        P(("row", "col"), None),
        P("col", "row", None),
        P(),
        P(),
        P(),
        P(),
        P(),
        P("col", None),
        P("row", "col", None, None),
        P("row", "col"),
        P("row", "col", None, None, None),
    )
    out_specs = P(("row", "col"), None)
    nrow, ncol = mesh.shape["row"], mesh.shape["col"]
    program = functools.partial(body, NX, nrow // NX, ncol)
    return jax.shard_map(program, mesh=mesh, in_specs=in_specs, out_specs=out_specs, check_vma=False)
```

```python
import functools
import math

import jax
import jax.numpy as jnp
from jax import lax
from jax.experimental import pallas as pl
from jax.experimental.pallas import tpu as pltpu
from jax.sharding import PartitionSpec as P

MASKED = -1e30
UNROLL = 16
BATCH = 8
CHUNKS = 8


def dot_nt(a, b):
    return lax.dot_general(a, b, (((1,), (1,)), ((), ())), preferred_element_type=jnp.float32)


MESH = pl.DeviceIdType.MESH
LINKS = ("x+", "x-", "z+", "z-")
STEP = {"x+": (1, 0), "x-": (-1, 0), "z+": (0, 1), "z-": (0, -1)}
SPLIT = 96


def spread_plan(nx, nz, rows):
    cut = {"A": (0, SPLIT // 2, SPLIT), "B": (SPLIT, (SPLIT + rows) // 2, rows)}
    sends, events, free, pending = [], [], {link: 0.0 for link in LINKS}, []

    def issue(now, kind, link, ox, oz, lo, hi):
        if hi <= lo:
            return
        start = max(free[link], now)
        free[link] = start + (hi - lo)
        pending.append((free[link] + 60.0, len(sends), kind))
        sends.append((link, ox, oz, lo, hi - lo))
        events.append(("send", len(sends) - 1))

    def clip(kind, link, k, half, lo, hi):
        if k + 1 < half:
            return lo, hi
        if k + 1 > half:
            return lo, lo
        a, m, b = cut[kind]
        return (max(lo, a), min(hi, m)) if link[1] == "+" else (max(lo, m), min(hi, b))

    for kind, order in (("B", ("z+", "z-")), ("A", ("x+", "x-")), ("A", ("z+", "z-")), ("B", ("x+", "x-"))):
        for link in order:
            issue(0.0, kind, link, 0, 0, cut[kind][0], cut[kind][2])
    while pending:
        pending.sort()
        now, k, kind = pending.pop(0)
        link, ox, oz, lo, n = sends[k]
        hi = lo + n
        events.append(("recv", k))
        ox, oz = ox - STEP[link][0], oz - STEP[link][1]
        on_x = link[0] == "x"
        first = on_x == (kind == "A")
        far, half = (abs(ox), nx // 2) if on_x else (abs(oz), nz // 2)
        a, b = clip(kind, link, far, half, lo, hi)
        issue(now, kind, link, ox, oz, a, b)
        if first:
            for other in ("z+", "z-") if on_x else ("x+", "x-"):
                a, b = clip(kind, other, 0, nz // 2 if on_x else nx // 2, lo, hi)
                issue(now, kind, other, ox, oz, a, b)
    return sends, events


def gather_kernel(
    nx, nz, ncol, sends, events,
    x_dst_hbm, w_query_hbm, x_src, mask_hbm,
    x_all, q_all, bias_hbm,
    x_dst, w_query, q_own, masks, bias, send_sem, recv_sem, q_send, q_recv, in_sem, out_sem, own_sem,
):
    row, col = lax.axis_index("row"), lax.axis_index("col")
    z, x = row // nx, lax.rem(row, nx)
    slots = masks.shape[0]
    chunks = in_sem.shape[0]
    per = slots // chunks

    def loaded(i):
        part = pl.ds(i * per, per)
        return pltpu.make_async_copy(mask_hbm.at[part], masks.at[part], in_sem.at[i])

    def stored(i):
        part = pl.ds(i * per, per)
        return pltpu.make_async_copy(bias.at[part], bias_hbm.at[part], out_sem.at[i])

    def at(ox, oz):
        return lax.rem(z + oz + nz, nz) * nx + lax.rem(x + ox + nx, nx)

    def peer(o):
        return lax.rem(col + o, ncol)

    barrier = pltpu.get_barrier_semaphore()
    for link in LINKS:
        pl.semaphore_signal(barrier, inc=1, device_id={"row": at(*STEP[link])}, device_id_type=MESH)
    for o in range(1, ncol):
        pl.semaphore_signal(barrier, inc=1, device_id={"col": peer(o)}, device_id_type=MESH)
    operands = [
        pltpu.make_async_copy(x_dst_hbm, x_dst, own_sem.at[2]),
        pltpu.make_async_copy(w_query_hbm, w_query, own_sem.at[3]),
    ]
    for copy in operands:
        copy.start()
    for i in range(chunks):
        loaded(i).start()
    own_x = pltpu.make_async_copy(x_src, x_all.at[row], own_sem.at[0])
    own_x.start()
    pl.semaphore_wait(barrier, len(LINKS) + ncol - 1)

    def piece(k, arriving):
        link, ox, oz, lo, n = sends[k]
        dx, dz = STEP[link]
        origin = at(ox - dx, oz - dz) if arriving else at(ox, oz)
        part = pl.ds(lo, n)
        own = ox == 0 and oz == 0 and not arriving
        return pltpu.make_async_remote_copy(
            src_ref=x_src.at[part] if own else x_all.at[origin, part],
            dst_ref=x_all.at[origin, part],
            send_sem=send_sem.at[k],
            recv_sem=recv_sem.at[k],
            device_id={"row": at(dx, dz)},
            device_id_type=MESH,
        )

    def query(o, slot):
        return pltpu.make_async_remote_copy(
            src_ref=q_own,
            dst_ref=q_all.at[slot],
            send_sem=q_send.at[o - 1],
            recv_sem=q_recv.at[o - 1],
            device_id={"col": peer(o)},
            device_id_type=MESH,
        )

    share = -(-slots // (len(sends) - 8))

    def turn(first, last):
        @pl.loop(first, last)
        def _(t):
            bias[t] = jnp.where(masks[t] == 1, 0.0, MASKED).T.astype(jnp.bfloat16)

    def work(first, last):
        for i in range(chunks):
            if first <= i * per < last:
                loaded(i).wait()
        turn(first, last)
        for i in range(chunks):
            if first < (i + 1) * per <= last:
                stored(i).start()

    own_q = None
    done = 0
    for n, (what, k) in enumerate(events):
        if what == "send":
            piece(k, False).start()
        else:
            if own_q is None:
                for copy in operands:
                    copy.wait()
                q = jnp.dot(x_dst[...], w_query[...], preferred_element_type=jnp.float32)
                q_own[...] = q.T.astype(jnp.bfloat16)
                for o in range(1, ncol):
                    query(o, col).start()
                own_q = pltpu.make_async_copy(q_own, q_all.at[col], own_sem.at[1])
                own_q.start()
            piece(k, True).wait_recv()
        if own_q is not None and done < slots and events[n + 1][0] == "recv":
            end = min(slots, done + share)
            work(done, end)
            done = end
    for o in range(1, ncol):
        query(o, lax.rem(col - o + ncol, ncol)).wait_recv()
    for k in range(len(sends)):
        piece(k, False).wait_send()
    for o in range(1, ncol):
        query(o, col).wait_send()
    for i in range(chunks):
        stored(i).wait()
    own_x.wait()
    own_q.wait()


def gather_all(nx, nz, ncol, x_dst, w_query, x_src, mask):
    rows, width = x_src.shape
    slots, tile, _ = mask.shape
    sends, events = spread_plan(nx, nz, rows)
    hbm = pl.BlockSpec(memory_space=pltpu.HBM)
    dma = pltpu.SemaphoreType.DMA
    return pl.pallas_call(
        functools.partial(gather_kernel, nx, nz, ncol, sends, events),
        out_shape=(
            jax.ShapeDtypeStruct((nx * nz, rows, width), jnp.bfloat16),
            jax.ShapeDtypeStruct((ncol, width, x_dst.shape[0]), jnp.bfloat16),
            jax.ShapeDtypeStruct(mask.shape, jnp.bfloat16),
        ),
        in_specs=[hbm, hbm, hbm, hbm],
        out_specs=(hbm, hbm, hbm),
        scratch_shapes=[
            pltpu.VMEM(x_dst.shape, jnp.bfloat16),
            pltpu.VMEM(w_query.shape, jnp.bfloat16),
            pltpu.VMEM((width, x_dst.shape[0]), jnp.bfloat16),
            pltpu.VMEM(mask.shape, jnp.int32),
            pltpu.VMEM(mask.shape, jnp.bfloat16),
            dma((len(sends),)),
            dma((len(sends),)),
            dma((ncol - 1,)),
            dma((ncol - 1,)),
            dma((16,)),
            dma((16,)),
            dma((4,)),
        ],
        compiler_params=pltpu.CompilerParams(
            collective_id=0, has_side_effects=True, vmem_limit_bytes=58 * 2**20
        ),
        name="gather_all",
    )(x_dst, w_query, x_src, mask)


def attend_kernel(
    coords_ref, count_ref, sink_ref, order_hbm, x_hbm, q_hbm, wk_hbm, wv_hbm, bias_hbm,
    acc_out, stat_out,
    order_ref, x_ref, q_ref, wk_ref, wv_ref, rows, picked, keys, values, qz, acc, top, total, bias, sbuf, peak,
    x_sem, sem,
):
    heads = sink_ref.shape[0]
    n_dblk, width, tile = q_hbm.shape
    hd = width // heads
    half = width // 2
    per_half = heads // 2
    c = math.log2(math.e) / math.sqrt(hd)
    nsrc = x_hbm.shape[0]
    nblk = nsrc // tile
    slots = bias_hbm.shape[0]
    count = count_ref[0, 0]
    part = nsrc // CHUNKS

    def x_load(i):
        r = pl.ds(i * part, part)
        return pltpu.make_async_copy(x_hbm.at[r], x_ref.at[r], x_sem.at[i])

    loads = [
        pltpu.make_async_copy(src, dst, sem.at[i])
        for i, (src, dst) in enumerate(
            (
                (q_hbm, q_ref),
                (order_hbm, order_ref),
                (wk_hbm, wk_ref),
                (wv_hbm, wv_ref),
                (bias_hbm, bias.at[pl.ds(0, slots)]),
            )
        )
    ]
    for load in loads[:1]:
        load.start()
    for i in range(CHUNKS):
        x_load(i).start()
    for load in loads[1:]:
        load.start()

    qz[...] = jnp.zeros_like(qz)
    loads[0].wait()
    for d in range(n_dblk):
        for h in range(heads):
            hh = h % per_half
            qz[d, hh * hd:(hh + 1) * hd, h * tile:(h + 1) * tile] = q_ref[d, h * hd:(h + 1) * hd, :]

    bias[slots] = jnp.full(bias.shape[1:], MASKED, jnp.bfloat16)
    acc[...] = jnp.zeros_like(acc)
    total[...] = jnp.zeros_like(total)
    for d in range(n_dblk):
        for h in range(heads):
            top[d, h:h + 1, :] = jnp.full((1, tile), sink_ref[h] * math.sqrt(hd), jnp.float32)

    for i in range(CHUNKS):
        x_load(i).wait()

        @pl.loop(0, part // 256)
        def _(j):
            first = pl.multiple_of(i * part + j * 256, 256)
            v = x_ref[pl.ds(first, 256), :].astype(jnp.float32)
            rows[pl.ds(2 * first, 256, stride=2), :] = v[:, :half]
            rows[pl.ds(2 * first + 1, 256, stride=2), :] = v[:, half:]

    for load in loads[1:4]:
        load.wait()
    wk = wk_ref[...]
    wvt = wv_ref[...].astype(jnp.float32).T.astype(jnp.bfloat16)
    batch = BATCH * tile

    @pl.loop(0, nblk // BATCH)
    def _(i):
        for r in range(batch):
            idx = order_ref[i * batch + r]
            picked[2 * r:2 * r + 2, :] = rows[pl.ds(pl.multiple_of(2 * idx, 2), 2), :]
        lo = picked[pl.ds(0, batch, stride=2), :].astype(jnp.bfloat16)
        hi = picked[pl.ds(1, batch, stride=2), :].astype(jnp.bfloat16)
        x = jnp.concatenate([lo, hi], axis=1)
        k = jnp.dot(x, wk, preferred_element_type=jnp.float32).astype(jnp.bfloat16)
        v = dot_nt(wvt, x).astype(jnp.bfloat16)
        for j in range(BATCH):
            keys[i * BATCH + j] = k[j * tile:(j + 1) * tile]
            values[i * BATCH + j] = v[:, j * tile:(j + 1) * tile]

    loads[4].wait()
    ones = jnp.ones((16, tile), jnp.bfloat16)

    def place(t):
        u = jnp.minimum(t, slots - 1)
        return coords_ref[0, u], coords_ref[1, u]

    def scores(t, e):
        d, b = place(t)
        bt = bias[jnp.where(t < count, t, slots)].astype(jnp.float32)
        for hp in range(heads // 2):
            g = 2 * hp // per_half
            pair = jnp.dot(
                keys[b, :, g * half:(g + 1) * half],
                qz[d, :, 2 * hp * tile:2 * (hp + 1) * tile],
                preferred_element_type=jnp.float32,
            )
            for i in range(2):
                s = pair[:, i * tile:(i + 1) * tile] + bt
                sbuf[e, 2 * hp + i] = s
                peak[e, 2 * hp + i:2 * hp + i + 1, :] = jnp.max(s, axis=0, keepdims=True)

    def weigh(t, e):
        d, b = place(t)
        before = top[d]
        now = jnp.maximum(before, peak[e])
        fade = jnp.exp2((before - now) * c)
        top[d] = now
        sums = []
        for h in range(heads):
            f = slice(h * hd, (h + 1) * hd)
            p = jnp.exp2((sbuf[e, h] - now[h:h + 1]) * c).astype(jnp.bfloat16)
            v = jnp.concatenate([values[b, f, :], ones], axis=0)
            o = jnp.dot(v, p, preferred_element_type=jnp.float32)
            acc[d, f, :] = acc[d, f, :] * fade[h:h + 1] + o[:hd]
            sums.append(o[hd:hd + 1])
        total[d] = total[d] * fade + jnp.concatenate(sums, axis=0)

    scores(0, 0)

    @pl.loop(0, (count + UNROLL - 1) // UNROLL)
    def _(i):
        for u in range(UNROLL):
            t = i * UNROLL + u
            scores(t + 1, (u + 1) % 2)
            weigh(t, u % 2)

    acc_out[...] = acc[...].astype(jnp.bfloat16)
    for d in range(n_dblk):
        stat_out[d, :heads, :] = top[d] * c
        stat_out[d, heads:, :] = total[d]


def attend(order, coords, count, sink, x, q, wk, wv, bias):
    nsrc, width = x.shape
    n_dblk, _, tile = q.shape
    heads = sink.shape[0]
    slots = bias.shape[0]
    nblk = nsrc // tile
    smem = pl.BlockSpec(memory_space=pltpu.SMEM)
    vmem = pl.BlockSpec(memory_space=pltpu.VMEM)
    hbm = pl.BlockSpec(memory_space=pltpu.HBM)
    return pl.pallas_call(
        attend_kernel,
        out_shape=(
            jax.ShapeDtypeStruct((n_dblk, width, tile), jnp.bfloat16),
            jax.ShapeDtypeStruct((n_dblk, 2 * heads, tile), jnp.float32),
        ),
        in_specs=[smem] * 3 + [hbm] * 6,
        out_specs=(vmem, vmem),
        scratch_shapes=[
            pltpu.SMEM((nsrc,), jnp.int32),
            pltpu.VMEM((nsrc, width), jnp.bfloat16),
            pltpu.VMEM(q.shape, jnp.bfloat16),
            pltpu.VMEM((width, width), jnp.bfloat16),
            pltpu.VMEM((width, width), jnp.bfloat16),
            pltpu.VMEM((2 * nsrc, width // 2), jnp.float32),
            pltpu.VMEM((2 * BATCH * tile, width // 2), jnp.float32),
            pltpu.VMEM((nblk, tile, width), jnp.bfloat16),
            pltpu.VMEM((nblk, width, tile), jnp.bfloat16),
            pltpu.VMEM((n_dblk, width // 2, heads * tile), jnp.bfloat16),
            pltpu.VMEM((n_dblk, width, tile), jnp.float32),
            pltpu.VMEM((n_dblk, heads, tile), jnp.float32),
            pltpu.VMEM((n_dblk, heads, tile), jnp.float32),
            pltpu.VMEM((slots + 1, tile, tile), jnp.bfloat16),
            pltpu.VMEM((2, heads, tile, tile), jnp.float32),
            pltpu.VMEM((2, heads, tile), jnp.float32),
            pltpu.SemaphoreType.DMA((CHUNKS,)),
            pltpu.SemaphoreType.DMA((5,)),
        ],
        compiler_params=pltpu.CompilerParams(vmem_limit_bytes=58 * 2**20),
        name="attend",
    )(coords, count, sink, order, x, q, wk, wv, bias)


def finish_kernel(
    ncol,
    sink_ref, acc_ref, stat_ref, w_out_hbm,
    out_ref,
    accs, stats, acc_own, stat_own, w_out, a_send, a_recv, s_send, s_recv, own_sem,
):
    col = lax.axis_index("col")
    heads = sink_ref.shape[0]
    _, width, tile = acc_ref.shape
    hd = width // heads

    def peer(o):
        return lax.rem(col + o, ncol)

    barrier = pltpu.get_barrier_semaphore()
    for o in range(1, ncol):
        pl.semaphore_signal(barrier, inc=1, device_id={"col": peer(o)}, device_id_type=MESH)
    own = [
        pltpu.make_async_copy(stat_ref.at[col], stat_own, own_sem.at[0]),
        pltpu.make_async_copy(acc_ref.at[col], acc_own, own_sem.at[1]),
        pltpu.make_async_copy(w_out_hbm, w_out, own_sem.at[2]),
    ]
    for load in own:
        load.start()
    pl.semaphore_wait(barrier, ncol - 1)

    moves = ((stat_ref, stats, s_send, s_recv), (acc_ref, accs, a_send, a_recv))

    def copy(o, which):
        src, dst, send, recv = moves[which]
        return pltpu.make_async_remote_copy(
            src_ref=src.at[peer(o)],
            dst_ref=dst.at[o - 1],
            send_sem=send.at[o - 1],
            recv_sem=recv.at[o - 1],
            device_id={"col": peer(o)},
            device_id_type=MESH,
        )

    order = sorted(range(1, ncol), key=lambda o: -min(o, ncol - o))
    for o in order:
        copy(o, 0).start()
        copy(o, 1).start()
    for load in own:
        load.wait()
    stat = [stat_own[...]]
    for o in range(1, ncol):
        copy(o, 0).wait_recv()
        stat.append(stats[o - 1])
    top = functools.reduce(jnp.maximum, [s[:heads] for s in stat])
    fades = [jnp.exp2(s[:heads] - top) for s in stat]
    sinks = jnp.concatenate([jnp.full((1, tile), sink_ref[h] * math.log2(math.e), jnp.float32) for h in range(heads)], axis=0)
    total = jnp.exp2(sinks - top)
    for s, fade in zip(stat, fades):
        total = total + s[heads:] * fade

    def spread(per_head):
        return jnp.concatenate([jnp.broadcast_to(per_head[h:h + 1], (hd, tile)) for h in range(heads)], axis=0)

    mixed = acc_own[...].astype(jnp.float32) * spread(fades[0])
    for o in range(1, ncol):
        copy(o, 1).wait_recv()
        mixed = mixed + accs[o - 1].astype(jnp.float32) * spread(fades[o])
    mixed = (mixed / spread(total)).T.astype(jnp.bfloat16)
    out_ref[...] = jnp.dot(mixed, w_out[...], preferred_element_type=jnp.float32).astype(jnp.bfloat16)
    for o in range(1, ncol):
        copy(o, 0).wait_send()
        copy(o, 1).wait_send()


def finish(sink, acc, stat, w_out):
    ncol, width, tile = acc.shape
    hbm = pl.BlockSpec(memory_space=pltpu.HBM)
    dma = pltpu.SemaphoreType.DMA
    return pl.pallas_call(
        functools.partial(finish_kernel, ncol),
        out_shape=jax.ShapeDtypeStruct((tile, width), jnp.bfloat16),
        in_specs=[pl.BlockSpec(memory_space=pltpu.SMEM), hbm, hbm, hbm],
        out_specs=pl.BlockSpec(memory_space=pltpu.VMEM),
        scratch_shapes=[
            pltpu.VMEM((ncol - 1, width, tile), jnp.bfloat16),
            pltpu.VMEM((ncol - 1,) + stat.shape[1:], jnp.float32),
            pltpu.VMEM((width, tile), jnp.bfloat16),
            pltpu.VMEM(stat.shape[1:], jnp.float32),
            pltpu.VMEM(w_out.shape, jnp.bfloat16),
        ]
        + [dma((ncol - 1,))] * 4
        + [dma((3,))],
        compiler_params=pltpu.CompilerParams(
            collective_id=1, has_side_effects=True, vmem_limit_bytes=58 * 2**20
        ),
        name="finish",
    )(sink, acc, stat, w_out)


def body(
    nx, nz, ncol,
    x_dst, x_src, w_query, w_key, w_value, w_out, sink, node_order, tile_coords, tile_count, edge_mask,
):
    x, q, bias = gather_all(nx, nz, ncol, x_dst, w_query, x_src[0], edge_mask[0, 0])
    acc, stat = attend(
        node_order[0], tile_coords[0, 0], tile_count, sink, x.reshape(-1, x.shape[-1]), q, w_key, w_value, bias
    )
    return finish(sink, acc, stat, w_out)


NX = 4


def solution(mesh):
    in_specs = (
        P(("row", "col"), None),
        P("col", "row", None),
        P(),
        P(),
        P(),
        P(),
        P(),
        P("col", None),
        P("row", "col", None, None),
        P("row", "col"),
        P("row", "col", None, None, None),
    )
    out_specs = P(("row", "col"), None)
    nrow, ncol = mesh.shape["row"], mesh.shape["col"]
    program = functools.partial(body, NX, nrow // NX, ncol)
    return jax.shard_map(program, mesh=mesh, in_specs=in_specs, out_specs=out_specs, check_vma=False)
```

```python
import functools
import math

import jax
import jax.numpy as jnp
from jax import lax
from jax.experimental import pallas as pl
from jax.experimental.pallas import tpu as pltpu
from jax.sharding import PartitionSpec as P

MASKED = -1e30
UNROLL = 32
BATCH = 8
CHUNKS = 8


def dot_nt(a, b):
    return lax.dot_general(a, b, (((1,), (1,)), ((), ())), preferred_element_type=jnp.float32)


MESH = pl.DeviceIdType.MESH
LINKS = ("x+", "x-", "z+", "z-")
STEP = {"x+": (1, 0), "x-": (-1, 0), "z+": (0, 1), "z-": (0, -1)}
SPLIT = 96


def spread_plan(nx, nz, rows):
    cut = {"A": (0, SPLIT // 2, SPLIT), "B": (SPLIT, (SPLIT + rows) // 2, rows)}
    sends, events, free, pending = [], [], {link: 0.0 for link in LINKS}, []

    def issue(now, kind, link, ox, oz, lo, hi):
        if hi <= lo:
            return
        start = max(free[link], now)
        free[link] = start + (hi - lo)
        pending.append((free[link] + 60.0, len(sends), kind))
        sends.append((link, ox, oz, lo, hi - lo))
        events.append(("send", len(sends) - 1))

    def clip(kind, link, k, half, lo, hi):
        if k + 1 < half:
            return lo, hi
        if k + 1 > half:
            return lo, lo
        a, m, b = cut[kind]
        return (max(lo, a), min(hi, m)) if link[1] == "+" else (max(lo, m), min(hi, b))

    for kind, order in (("B", ("z+", "z-")), ("A", ("x+", "x-")), ("A", ("z+", "z-")), ("B", ("x+", "x-"))):
        for link in order:
            issue(0.0, kind, link, 0, 0, cut[kind][0], cut[kind][2])
    while pending:
        pending.sort()
        now, k, kind = pending.pop(0)
        link, ox, oz, lo, n = sends[k]
        hi = lo + n
        events.append(("recv", k))
        ox, oz = ox - STEP[link][0], oz - STEP[link][1]
        on_x = link[0] == "x"
        first = on_x == (kind == "A")
        far, half = (abs(ox), nx // 2) if on_x else (abs(oz), nz // 2)
        a, b = clip(kind, link, far, half, lo, hi)
        issue(now, kind, link, ox, oz, a, b)
        if first:
            for other in ("z+", "z-") if on_x else ("x+", "x-"):
                a, b = clip(kind, other, 0, nz // 2 if on_x else nx // 2, lo, hi)
                issue(now, kind, other, ox, oz, a, b)
    return sends, events


def gather_kernel(
    nx, nz, ncol, sends, events,
    x_dst_hbm, w_query_hbm, x_src, mask_hbm,
    x_all, q_all, bias_hbm,
    x_dst, w_query, q_own, masks, bias, send_sem, recv_sem, q_send, q_recv, in_sem, out_sem, own_sem,
):
    row, col = lax.axis_index("row"), lax.axis_index("col")
    z, x = row // nx, lax.rem(row, nx)
    slots = masks.shape[0]
    chunks = in_sem.shape[0]
    per = slots // chunks

    def loaded(i):
        part = pl.ds(i * per, per)
        return pltpu.make_async_copy(mask_hbm.at[part], masks.at[part], in_sem.at[i])

    def stored(i):
        part = pl.ds(i * per, per)
        return pltpu.make_async_copy(bias.at[part], bias_hbm.at[part], out_sem.at[i])

    def at(ox, oz):
        return lax.rem(z + oz + nz, nz) * nx + lax.rem(x + ox + nx, nx)

    def peer(o):
        return lax.rem(col + o, ncol)

    barrier = pltpu.get_barrier_semaphore()
    for link in LINKS:
        pl.semaphore_signal(barrier, inc=1, device_id={"row": at(*STEP[link])}, device_id_type=MESH)
    for o in range(1, ncol):
        pl.semaphore_signal(barrier, inc=1, device_id={"col": peer(o)}, device_id_type=MESH)
    operands = [
        pltpu.make_async_copy(x_dst_hbm, x_dst, own_sem.at[2]),
        pltpu.make_async_copy(w_query_hbm, w_query, own_sem.at[3]),
    ]
    for copy in operands:
        copy.start()
    for i in range(chunks):
        loaded(i).start()
    own_x = pltpu.make_async_copy(x_src, x_all.at[row], own_sem.at[0])
    own_x.start()
    pl.semaphore_wait(barrier, len(LINKS) + ncol - 1)

    def piece(k, arriving):
        link, ox, oz, lo, n = sends[k]
        dx, dz = STEP[link]
        origin = at(ox - dx, oz - dz) if arriving else at(ox, oz)
        part = pl.ds(lo, n)
        own = ox == 0 and oz == 0 and not arriving
        return pltpu.make_async_remote_copy(
            src_ref=x_src.at[part] if own else x_all.at[origin, part],
            dst_ref=x_all.at[origin, part],
            send_sem=send_sem.at[k],
            recv_sem=recv_sem.at[k],
            device_id={"row": at(dx, dz)},
            device_id_type=MESH,
        )

    def query(o, slot):
        return pltpu.make_async_remote_copy(
            src_ref=q_own,
            dst_ref=q_all.at[slot],
            send_sem=q_send.at[o - 1],
            recv_sem=q_recv.at[o - 1],
            device_id={"col": peer(o)},
            device_id_type=MESH,
        )

    share = -(-slots // (len(sends) - 8))

    def turn(first, last):
        @pl.loop(first, last)
        def _(t):
            bias[t] = jnp.where(masks[t] == 1, 0.0, MASKED).T.astype(jnp.bfloat16)

    def work(first, last):
        for i in range(chunks):
            if first <= i * per < last:
                loaded(i).wait()
        turn(first, last)
        for i in range(chunks):
            if first < (i + 1) * per <= last:
                stored(i).start()

    own_q = None
    done = 0
    for n, (what, k) in enumerate(events):
        if what == "send":
            piece(k, False).start()
        else:
            if own_q is None:
                for copy in operands:
                    copy.wait()
                q = jnp.dot(x_dst[...], w_query[...], preferred_element_type=jnp.float32)
                q_own[...] = q.T.astype(jnp.bfloat16)
                for o in range(1, ncol):
                    query(o, col).start()
                own_q = pltpu.make_async_copy(q_own, q_all.at[col], own_sem.at[1])
                own_q.start()
            piece(k, True).wait_recv()
        if own_q is not None and done < slots and events[n + 1][0] == "recv":
            end = min(slots, done + share)
            work(done, end)
            done = end
    for o in range(1, ncol):
        query(o, lax.rem(col - o + ncol, ncol)).wait_recv()
    for k in range(len(sends)):
        piece(k, False).wait_send()
    for o in range(1, ncol):
        query(o, col).wait_send()
    for i in range(chunks):
        stored(i).wait()
    own_x.wait()
    own_q.wait()


def gather_all(nx, nz, ncol, x_dst, w_query, x_src, mask):
    rows, width = x_src.shape
    slots, tile, _ = mask.shape
    sends, events = spread_plan(nx, nz, rows)
    hbm = pl.BlockSpec(memory_space=pltpu.HBM)
    dma = pltpu.SemaphoreType.DMA
    return pl.pallas_call(
        functools.partial(gather_kernel, nx, nz, ncol, sends, events),
        out_shape=(
            jax.ShapeDtypeStruct((nx * nz, rows, width), jnp.bfloat16),
            jax.ShapeDtypeStruct((ncol, width, x_dst.shape[0]), jnp.bfloat16),
            jax.ShapeDtypeStruct(mask.shape, jnp.bfloat16),
        ),
        in_specs=[hbm, hbm, hbm, hbm],
        out_specs=(hbm, hbm, hbm),
        scratch_shapes=[
            pltpu.VMEM(x_dst.shape, jnp.bfloat16),
            pltpu.VMEM(w_query.shape, jnp.bfloat16),
            pltpu.VMEM((width, x_dst.shape[0]), jnp.bfloat16),
            pltpu.VMEM(mask.shape, jnp.int32),
            pltpu.VMEM(mask.shape, jnp.bfloat16),
            dma((len(sends),)),
            dma((len(sends),)),
            dma((ncol - 1,)),
            dma((ncol - 1,)),
            dma((16,)),
            dma((16,)),
            dma((4,)),
        ],
        compiler_params=pltpu.CompilerParams(
            collective_id=0, has_side_effects=True, vmem_limit_bytes=58 * 2**20
        ),
        name="gather_all",
    )(x_dst, w_query, x_src, mask)


def attend_kernel(
    coords_ref, count_ref, sink_ref, order_hbm, x_hbm, q_hbm, wk_hbm, wv_hbm, bias_hbm,
    acc_out, stat_out,
    order_ref, x_ref, q_ref, wk_ref, wv_ref, rows, picked, keys, values, qz, acc, top, total, bias, sbuf, peak,
    x_sem, sem,
):
    heads = sink_ref.shape[0]
    n_dblk, width, tile = q_hbm.shape
    hd = width // heads
    half = width // 2
    per_half = heads // 2
    c = math.log2(math.e) / math.sqrt(hd)
    nsrc = x_hbm.shape[0]
    nblk = nsrc // tile
    slots = bias_hbm.shape[0]
    count = count_ref[0, 0]
    part = nsrc // CHUNKS

    def x_load(i):
        r = pl.ds(i * part, part)
        return pltpu.make_async_copy(x_hbm.at[r], x_ref.at[r], x_sem.at[i])

    loads = [
        pltpu.make_async_copy(src, dst, sem.at[i])
        for i, (src, dst) in enumerate(
            (
                (q_hbm, q_ref),
                (order_hbm, order_ref),
                (wk_hbm, wk_ref),
                (wv_hbm, wv_ref),
                (bias_hbm, bias.at[pl.ds(0, slots)]),
            )
        )
    ]
    for load in loads[:1]:
        load.start()
    for i in range(CHUNKS):
        x_load(i).start()
    for load in loads[1:]:
        load.start()

    qz[...] = jnp.zeros_like(qz)
    loads[0].wait()
    for d in range(n_dblk):
        for h in range(heads):
            hh = h % per_half
            qz[d, hh * hd:(hh + 1) * hd, h * tile:(h + 1) * tile] = q_ref[d, h * hd:(h + 1) * hd, :]

    bias[slots] = jnp.full(bias.shape[1:], MASKED, jnp.bfloat16)
    acc[...] = jnp.zeros_like(acc)
    total[...] = jnp.zeros_like(total)
    for d in range(n_dblk):
        for h in range(heads):
            top[d, h:h + 1, :] = jnp.full((1, tile), sink_ref[h] * math.sqrt(hd), jnp.float32)

    for i in range(CHUNKS):
        x_load(i).wait()

        @pl.loop(0, part // 256)
        def _(j):
            first = pl.multiple_of(i * part + j * 256, 256)
            v = x_ref[pl.ds(first, 256), :].astype(jnp.float32)
            rows[pl.ds(2 * first, 256, stride=2), :] = v[:, :half]
            rows[pl.ds(2 * first + 1, 256, stride=2), :] = v[:, half:]

    for load in loads[1:4]:
        load.wait()
    wk = wk_ref[...]
    wvt = wv_ref[...].astype(jnp.float32).T.astype(jnp.bfloat16)
    batch = BATCH * tile

    @pl.loop(0, nblk // BATCH)
    def _(i):
        for r in range(batch):
            idx = order_ref[i * batch + r]
            picked[2 * r:2 * r + 2, :] = rows[pl.ds(pl.multiple_of(2 * idx, 2), 2), :]
        lo = picked[pl.ds(0, batch, stride=2), :].astype(jnp.bfloat16)
        hi = picked[pl.ds(1, batch, stride=2), :].astype(jnp.bfloat16)
        x = jnp.concatenate([lo, hi], axis=1)
        k = jnp.dot(x, wk, preferred_element_type=jnp.float32).astype(jnp.bfloat16)
        v = dot_nt(wvt, x).astype(jnp.bfloat16)
        for j in range(BATCH):
            keys[i * BATCH + j] = k[j * tile:(j + 1) * tile]
            values[i * BATCH + j] = v[:, j * tile:(j + 1) * tile]

    loads[4].wait()
    ones = jnp.ones((16, tile), jnp.bfloat16)

    def place(t):
        u = jnp.minimum(t, slots - 1)
        return coords_ref[0, u], coords_ref[1, u]

    def scores(e, hp, d, b, bt):
        g = 2 * hp // per_half
        pair = jnp.dot(
            keys[b, :, g * half:(g + 1) * half],
            qz[d, :, 2 * hp * tile:2 * (hp + 1) * tile],
            preferred_element_type=jnp.float32,
        )
        for i in range(2):
            s = pair[:, i * tile:(i + 1) * tile] + bt
            sbuf[e, 2 * hp + i] = s
            peak[e, 2 * hp + i:2 * hp + i + 1, :] = jnp.max(s, axis=0, keepdims=True)

    def terms(t):
        return bias[jnp.where(t < count, t, slots)].astype(jnp.float32)

    def step(t, e):
        d, b = place(t)
        dn, bn = place(t + 1)
        bt = terms(t + 1)
        before = top[d]
        now = jnp.maximum(before, peak[e])
        fade = jnp.exp2((before - now) * c)
        top[d] = now
        sums = []
        for hp in range(heads // 2):
            scores(1 - e, hp, dn, bn, bt)
            for h in (2 * hp, 2 * hp + 1):
                f = slice(h * hd, (h + 1) * hd)
                p = jnp.exp2((sbuf[e, h] - now[h:h + 1]) * c).astype(jnp.bfloat16)
                v = jnp.concatenate([values[b, f, :], ones], axis=0)
                o = jnp.dot(v, p, preferred_element_type=jnp.float32)
                acc[d, f, :] = acc[d, f, :] * fade[h:h + 1] + o[:hd]
                sums.append(o[hd:hd + 1])
        total[d] = total[d] * fade + jnp.concatenate(sums, axis=0)

    d0, b0 = place(0)
    for hp in range(heads // 2):
        scores(0, hp, d0, b0, terms(0))

    @pl.loop(0, (count + UNROLL - 1) // UNROLL)
    def _(i):
        for u in range(UNROLL):
            step(i * UNROLL + u, u % 2)

    acc_out[...] = acc[...].astype(jnp.bfloat16)
    for d in range(n_dblk):
        stat_out[d, :heads, :] = top[d] * c
        stat_out[d, heads:, :] = total[d]


def attend(order, coords, count, sink, x, q, wk, wv, bias):
    nsrc, width = x.shape
    n_dblk, _, tile = q.shape
    heads = sink.shape[0]
    slots = bias.shape[0]
    nblk = nsrc // tile
    smem = pl.BlockSpec(memory_space=pltpu.SMEM)
    vmem = pl.BlockSpec(memory_space=pltpu.VMEM)
    hbm = pl.BlockSpec(memory_space=pltpu.HBM)
    return pl.pallas_call(
        attend_kernel,
        out_shape=(
            jax.ShapeDtypeStruct((n_dblk, width, tile), jnp.bfloat16),
            jax.ShapeDtypeStruct((n_dblk, 2 * heads, tile), jnp.float32),
        ),
        in_specs=[smem] * 3 + [hbm] * 6,
        out_specs=(vmem, vmem),
        scratch_shapes=[
            pltpu.SMEM((nsrc,), jnp.int32),
            pltpu.VMEM((nsrc, width), jnp.bfloat16),
            pltpu.VMEM(q.shape, jnp.bfloat16),
            pltpu.VMEM((width, width), jnp.bfloat16),
            pltpu.VMEM((width, width), jnp.bfloat16),
            pltpu.VMEM((2 * nsrc, width // 2), jnp.float32),
            pltpu.VMEM((2 * BATCH * tile, width // 2), jnp.float32),
            pltpu.VMEM((nblk, tile, width), jnp.bfloat16),
            pltpu.VMEM((nblk, width, tile), jnp.bfloat16),
            pltpu.VMEM((n_dblk, width // 2, heads * tile), jnp.bfloat16),
            pltpu.VMEM((n_dblk, width, tile), jnp.float32),
            pltpu.VMEM((n_dblk, heads, tile), jnp.float32),
            pltpu.VMEM((n_dblk, heads, tile), jnp.float32),
            pltpu.VMEM((slots + 1, tile, tile), jnp.bfloat16),
            pltpu.VMEM((2, heads, tile, tile), jnp.float32),
            pltpu.VMEM((2, heads, tile), jnp.float32),
            pltpu.SemaphoreType.DMA((CHUNKS,)),
            pltpu.SemaphoreType.DMA((5,)),
        ],
        compiler_params=pltpu.CompilerParams(vmem_limit_bytes=58 * 2**20),
        name="attend",
    )(coords, count, sink, order, x, q, wk, wv, bias)


def finish_kernel(
    ncol,
    sink_ref, acc_ref, stat_ref, w_out_hbm,
    out_ref,
    accs, stats, acc_own, stat_own, w_out, a_send, a_recv, s_send, s_recv, own_sem,
):
    col = lax.axis_index("col")
    heads = sink_ref.shape[0]
    _, width, tile = acc_ref.shape
    hd = width // heads

    def peer(o):
        return lax.rem(col + o, ncol)

    barrier = pltpu.get_barrier_semaphore()
    for o in range(1, ncol):
        pl.semaphore_signal(barrier, inc=1, device_id={"col": peer(o)}, device_id_type=MESH)
    own = [
        pltpu.make_async_copy(stat_ref.at[col], stat_own, own_sem.at[0]),
        pltpu.make_async_copy(acc_ref.at[col], acc_own, own_sem.at[1]),
        pltpu.make_async_copy(w_out_hbm, w_out, own_sem.at[2]),
    ]
    for load in own:
        load.start()
    pl.semaphore_wait(barrier, ncol - 1)

    moves = ((stat_ref, stats, s_send, s_recv), (acc_ref, accs, a_send, a_recv))

    def copy(o, which):
        src, dst, send, recv = moves[which]
        return pltpu.make_async_remote_copy(
            src_ref=src.at[peer(o)],
            dst_ref=dst.at[o - 1],
            send_sem=send.at[o - 1],
            recv_sem=recv.at[o - 1],
            device_id={"col": peer(o)},
            device_id_type=MESH,
        )

    order = sorted(range(1, ncol), key=lambda o: -min(o, ncol - o))
    for o in order:
        copy(o, 0).start()
        copy(o, 1).start()
    for load in own:
        load.wait()
    stat = [stat_own[...]]
    for o in range(1, ncol):
        copy(o, 0).wait_recv()
        stat.append(stats[o - 1])
    top = functools.reduce(jnp.maximum, [s[:heads] for s in stat])
    fades = [jnp.exp2(s[:heads] - top) for s in stat]
    sinks = jnp.concatenate([jnp.full((1, tile), sink_ref[h] * math.log2(math.e), jnp.float32) for h in range(heads)], axis=0)
    total = jnp.exp2(sinks - top)
    for s, fade in zip(stat, fades):
        total = total + s[heads:] * fade

    def spread(per_head):
        return jnp.concatenate([jnp.broadcast_to(per_head[h:h + 1], (hd, tile)) for h in range(heads)], axis=0)

    mixed = acc_own[...].astype(jnp.float32) * spread(fades[0])
    for o in range(1, ncol):
        copy(o, 1).wait_recv()
        mixed = mixed + accs[o - 1].astype(jnp.float32) * spread(fades[o])
    mixed = (mixed / spread(total)).T.astype(jnp.bfloat16)
    out_ref[...] = jnp.dot(mixed, w_out[...], preferred_element_type=jnp.float32).astype(jnp.bfloat16)
    for o in range(1, ncol):
        copy(o, 0).wait_send()
        copy(o, 1).wait_send()


def finish(sink, acc, stat, w_out):
    ncol, width, tile = acc.shape
    hbm = pl.BlockSpec(memory_space=pltpu.HBM)
    dma = pltpu.SemaphoreType.DMA
    return pl.pallas_call(
        functools.partial(finish_kernel, ncol),
        out_shape=jax.ShapeDtypeStruct((tile, width), jnp.bfloat16),
        in_specs=[pl.BlockSpec(memory_space=pltpu.SMEM), hbm, hbm, hbm],
        out_specs=pl.BlockSpec(memory_space=pltpu.VMEM),
        scratch_shapes=[
            pltpu.VMEM((ncol - 1, width, tile), jnp.bfloat16),
            pltpu.VMEM((ncol - 1,) + stat.shape[1:], jnp.float32),
            pltpu.VMEM((width, tile), jnp.bfloat16),
            pltpu.VMEM(stat.shape[1:], jnp.float32),
            pltpu.VMEM(w_out.shape, jnp.bfloat16),
        ]
        + [dma((ncol - 1,))] * 4
        + [dma((3,))],
        compiler_params=pltpu.CompilerParams(
            collective_id=1, has_side_effects=True, vmem_limit_bytes=58 * 2**20
        ),
        name="finish",
    )(sink, acc, stat, w_out)


def body(
    nx, nz, ncol,
    x_dst, x_src, w_query, w_key, w_value, w_out, sink, node_order, tile_coords, tile_count, edge_mask,
):
    x, q, bias = gather_all(nx, nz, ncol, x_dst, w_query, x_src[0], edge_mask[0, 0])
    acc, stat = attend(
        node_order[0], tile_coords[0, 0], tile_count, sink, x.reshape(-1, x.shape[-1]), q, w_key, w_value, bias
    )
    return finish(sink, acc, stat, w_out)


NX = 4


def solution(mesh):
    in_specs = (
        P(("row", "col"), None),
        P("col", "row", None),
        P(),
        P(),
        P(),
        P(),
        P(),
        P("col", None),
        P("row", "col", None, None),
        P("row", "col"),
        P("row", "col", None, None, None),
    )
    out_specs = P(("row", "col"), None)
    nrow, ncol = mesh.shape["row"], mesh.shape["col"]
    program = functools.partial(body, NX, nrow // NX, ncol)
    return jax.shard_map(program, mesh=mesh, in_specs=in_specs, out_specs=out_specs, check_vma=False)
```
